32 devices in a mesh: groups: 2 (over y), seq: 4 (over z), dp: 2 (over x), sub: 2 (over core).
Axes of the slice: x: 2, y: 2, z: 4, core: 2. Of those that a mesh axis runs over, the one named last changes fastest.
Arguments:
- signal: bfloat16 [8, 2048, 512], P(('groups', 'dp', 'sub'), 'seq'), parts along dimension 0, may hold values from -6 to 6
- conv_weight: bfloat16 [512, 3, 1024], P(('dp', 'sub')), may hold values from -0.15625 to 0.15625
- proj_weight: bfloat16 [512, 512], P(('dp', 'sub')), may hold values from -0.25 to 0.25
- cotangent: bfloat16 [8, 2048, 512], P(('groups', 'dp', 'sub'), 'seq'), parts along dimension 0, may hold values from -6 to 6
Outputs:
- output: bfloat16 [8, 2048, 512], P(('groups', 'dp', 'sub'), 'seq'), parts along dimension 0
- grad_input: bfloat16 [8, 2048, 512], P(('groups', 'dp', 'sub'), 'seq'), parts along dimension 0
- grad_conv: float32 [1024, 3, 1024], P(('groups', 'dp', 'sub')), parts along dimension 0
- grad_proj: float32 [1024, 512], P(('groups', 'dp', 'sub')), parts along dimension 0
The draws below stay inside these ranges and needn't reach their ends.
There are 2 independent parts, one for each index of `groups`. The reference program is written for one: setup_inputs(seed, part) draws one part's arguments, and reference() takes and returns one part's arrays. A program takes and returns all parts, laid end to end along the dimension named above; an argument that names none is the same for every part. Nothing has to cross between parts.
All inputs are finite; a program needn't handle non-finite values.
Results may differ from the reference program's by a relative error of at most 0.012.
Values may be sent and summed in bfloat16 or wider, within the bound.
A program may use at most 64 MiB of HBM per device.

```python
import math
import jax
import jax.numpy as jnp
from jax import lax

CHANNELS = 512
DILATION = 512
ROWS = 512
STREAMS = 4
TIME = 2048
N_SEQ = 4


def raised(array, key, source, target, parts, factor):
    owner, partner = [(jnp.arange(array.shape[axis_at]) // (array.shape[axis_at] // parts)).reshape([-1 if axis == axis_at else 1 for axis in range(array.ndim)]) for axis_at in (source, target)]
    chosen = jax.random.permutation(key, parts)[partner]
    strong = (owner == chosen) | (owner == (partner + parts // 2) % parts)
    return jnp.where(strong, factor * array, array)


def shard_levels(stream_key, extent, split, low, high):
    factor_of = 1.0
    for position, blocks in split:
        heights = jax.random.uniform(jax.random.fold_in(jax.random.fold_in(stream_key, 6), position), (blocks,), jnp.float32, low / len(split), high / len(split))
        factor_of = factor_of * jnp.repeat(jnp.exp(heights), extent[position] // blocks).reshape((-1,) + (1,) * (len(extent) - 1 - position))
    return factor_of


def noise(stream_key, extent, scale, limit, split=(), kind=jnp.bfloat16):
    loudness = shard_levels(stream_key, extent, split, -0.22, 0.18) if split else 1.0
    array = jax.random.normal(stream_key, extent, jnp.float32) * scale * loudness
    return jnp.minimum(jnp.maximum(array, -limit), limit).astype(kind)


def bell_draw_with(key, dims, width, bound, split, heavy, held_as=jnp.bfloat16):
    entries = width * jax.random.normal(key, dims, jnp.float32)
    if split:
        entries = entries * shard_levels(key, dims, split, -0.22, 0.18)
    return jnp.clip(raised(entries, jax.random.fold_in(key, 3), *heavy), -bound, bound).astype(held_as)


def setup_inputs(seed: int = 0, part: int = 0) -> dict:
    key_of = jax.random.split(jax.random.key(seed), 5)
    part_keys = jax.random.split(jax.random.fold_in(key_of[4], part), 5)
    return {
        "signal": bell_draw_with(part_keys[0], (STREAMS, TIME, CHANNELS), 1.0, 6.0, ((0, 4), (1, 4)), (0, 2, 4, 2.0)),
        "conv_weight": noise(key_of[1], (CHANNELS, 3, 2 * CHANNELS), (3 * CHANNELS) ** -0.5, 0.15625, ((0, 4),)),
        "proj_weight": noise(key_of[2], (CHANNELS, CHANNELS), CHANNELS ** -0.5, 0.25, ((0, 4),)),
        "cotangent": bell_draw_with(part_keys[3], (STREAMS, TIME, CHANNELS), 1.0, 6.0, ((0, 4), (1, 4)), (1, 2, 4, 2.0)),
    }


def delayed(block, steps):
    if steps == 0:
        return block
    padding = jnp.zeros((steps, block.shape[1]), block.dtype)
    return jnp.concatenate([padding, block[:block.shape[0] - steps]], axis=0)

def advanced(block, steps):
    if steps == 0:
        return block
    padding = jnp.zeros((steps, block.shape[1]), block.dtype)
    return jnp.concatenate([block[steps:], padding], axis=0)

def segment_sums(left_side, right_side):
    left_blocks = left_side.astype(jnp.float32).reshape(N_SEQ, ROWS, left_side.shape[1])
    right_blocks = right_side.astype(jnp.float32).reshape(N_SEQ, ROWS, right_side.shape[1])
    partial_sums = jnp.einsum('sra,srb->sab', left_blocks, right_blocks, precision=lax.Precision.HIGHEST)
    rounded = lax.optimization_barrier(partial_sums.astype(jnp.bfloat16))
    return lax.optimization_barrier(jnp.sum(rounded.astype(jnp.float32), axis=0))

def reference(signal, conv_weight, proj_weight, cotangent):

    def one_stream(pair):
        stream_in, upstream = pair
        taps = [delayed(stream_in, tap_index * DILATION) for tap_index in range(3)]
        preact = jnp.dot(taps[0], conv_weight[:, 0, :], preferred_element_type=jnp.float32)
        for tap_index in range(1, 3):
            preact = preact + jnp.dot(taps[tap_index], conv_weight[:, tap_index, :], preferred_element_type=jnp.float32)
        tanh_part = jnp.tanh(preact[:, :CHANNELS])
        gate_part = jax.nn.sigmoid(preact[:, CHANNELS:])
        gated = (tanh_part * gate_part).astype(jnp.bfloat16)
        output = (stream_in.astype(jnp.float32) + jnp.dot(gated, proj_weight, preferred_element_type=jnp.float32)).astype(jnp.bfloat16)
        grad_gated = jnp.dot(upstream, proj_weight.T, preferred_element_type=jnp.float32)
        grad_pre = jnp.concatenate([grad_gated * gate_part * (1.0 - tanh_part * tanh_part), grad_gated * tanh_part * gate_part * (1.0 - gate_part)], axis=1).astype(jnp.bfloat16)
        back_sum = upstream.astype(jnp.float32)
        for tap_index in range(3):
            back_sum = back_sum + jnp.dot(advanced(grad_pre, tap_index * DILATION), conv_weight[:, tap_index, :].T, preferred_element_type=jnp.float32)
        grad_input = back_sum.astype(jnp.bfloat16)
        conv_part = jnp.stack([segment_sums(taps[tap_index], grad_pre) for tap_index in range(3)], axis=1)
        proj_part = segment_sums(gated, upstream)
        return (output, grad_input, conv_part, proj_part)
    output, grad_input, conv_parts, proj_parts = lax.map(one_stream, (signal, cotangent))
    factor = 1.0 / math.sqrt(STREAMS * TIME)
    grad_conv = lax.optimization_barrier(jnp.sum(conv_parts, axis=0)) * factor
    grad_proj = lax.optimization_barrier(jnp.sum(proj_parts, axis=0)) * factor
    return (output, grad_input, grad_conv, grad_proj)
```

```python
import functools
import math

import jax
import jax.numpy as jnp
from jax import lax
from jax.experimental import pallas as pl
from jax.experimental.pallas import tpu as pltpu
from jax.sharding import PartitionSpec as P

DILATION = 512
TAPS = 3
PIECES = 4
CHUNKS = 2
MESH = pl.DeviceIdType.MESH
F32 = jnp.float32
BF16 = jnp.bfloat16
NN = (((1,), (0,)), ((), ()))
NT = (((1,), (1,)), ((), ()))


def mm(a, b, dims=NN):
    return lax.dot_general(a, b, dims, preferred_element_type=F32)


def layer_kernel(
    sizes, factor,
    sig, cw, pw, cot,
    out, gin, gconv, gproj,
    sig1, sig2, sigt, gatedt, w, wp, gp, gated,
    p2in, p1in, p2out, p1out,
    grads, half_in, x_out, x_in, share, z_out, z_below, z_above, total,
    halo_s, halo_r, wx_s, wx_r, wy_s, wy_r, wc_s, wc_r,
    p_s, p_r, c_s, c_r, x_s, x_r, zb_s, zb_r, za_s, za_r, tu_s, td_s, t_r,
):
    ny, nz, nx, nc = sizes
    h, z, d, c = (lax.axis_index(name) for name in ("groups", "seq", "dp", "sub"))
    rows, chans = sig.shape
    part = cw.shape[1]
    cut = part // ny
    step = rows // CHUNKS
    reduce_time = nz == PIECES
    below, above = z > 0, z < nz - 1

    def copy(src, dst, send, recv, **where):
        return pltpu.make_async_remote_copy(
            src_ref=src, dst_ref=dst, send_sem=send, recv_sem=recv,
            device_id=where, device_id_type=MESH,
        )

    barrier = pltpu.get_barrier_semaphore()

    def greet(**where):
        pl.semaphore_signal(barrier, inc=1, device_id=where, device_id_type=MESH)

    @pl.when(below)
    def _():
        greet(seq=z - 1)

    @pl.when(above)
    def _():
        greet(seq=z + 1)

    for o in range(1, nx):
        greet(dp=lax.rem(d + o, nx))
    greet(sub=1 - c)
    greet(groups=1 - h)
    pl.semaphore_wait(
        barrier, (nx - 1) + 2 + below.astype(jnp.int32) + above.astype(jnp.int32)
    )

    def rows_of(j):
        return pl.ds(j * step, step)

    own_halo = [
        copy(sig.at[rows_of(j)], sig1.at[rows_of(j)], halo_s.at[0, j], halo_r.at[0, j], seq=z + 1)
        for j in range(CHUNKS)
    ]
    far_halo = [
        copy(sig1.at[rows_of(j)], sig2.at[rows_of(j)], halo_s.at[1, j], halo_r.at[1, j], seq=z + 1)
        for j in range(CHUNKS)
    ]

    @pl.when(above)
    def _():
        for j in range(CHUNKS):
            own_halo[j].start()

    def shard(k):
        return cw.at[k] if k < TAPS else pw

    def full(k, at, length):
        at = pl.ds(pl.multiple_of(at, 16), length)
        return w.at[k, at] if k < TAPS else wp.at[at]

    def base(dp_index):
        return (dp_index * nc + c) * part

    mine = base(d)
    wx, wy, wc = {}, {}, {}
    for k in range(TAPS + 1):
        for o in range(1, nx):
            wx[k, o] = copy(
                shard(k).at[pl.ds(pl.multiple_of(h * cut, 16), cut)], full(k, mine + h * cut, cut),
                wx_s.at[k, o], wx_r.at[k, o], dp=lax.rem(d + o, nx),
            )
            wx[k, o].start()
    for k in range(TAPS + 1):
        wc[k, 0, 0] = copy(
            shard(k), full(k, mine, part), wc_s.at[k, 0, 0], wc_r.at[k, 0, 0], sub=1 - c
        )
        wc[k, 0, 0].start()
    at_mine = pl.ds(pl.multiple_of(mine, 16), part)
    for k in range(TAPS):
        w[k, at_mine] = cw[k]
    wp[at_mine] = pw[...]

    @pl.when(z == 0)
    def _():
        sig1[...] = jnp.zeros_like(sig1)

    @pl.when(z < 2)
    def _():
        sig2[...] = jnp.zeros_like(sig2)

    @pl.when(z == nz - 1)
    def _():
        p2in[...] = jnp.zeros_like(p2in)
        p1in[...] = jnp.zeros_like(p1in)

    def pass_halo(j):
        @pl.when(below)
        def _():
            own_halo[j].wait_recv()

        @pl.when(below & above)
        def _():
            far_halo[j].start()

    for k in range(TAPS + 1):
        for o in range(1, nx):
            wx[k, o].wait_recv()
            region = full(k, base(lax.rem(d - o + nx, nx)) + h * cut, cut)
            wy[k, o] = copy(region, region, wy_s.at[k, o], wy_r.at[k, o], groups=1 - h)
            wy[k, o].start()
            wc[k, o, 0] = copy(region, region, wc_s.at[k, o, 0], wc_r.at[k, o, 0], sub=1 - c)
            wc[k, o, 0].start()
        if k < CHUNKS:
            pass_halo(k)
    sigt[0] = sig[...].T
    for k in range(TAPS + 1):
        for o in range(1, nx):
            wy[k, o].wait_recv()
            region = full(k, base(lax.rem(d - o + nx, nx)) + (1 - h) * cut, cut)
            wc[k, o, 1] = copy(region, region, wc_s.at[k, o, 1], wc_r.at[k, o, 1], sub=1 - c)
            wc[k, o, 1].start()
    for item in wc.values():
        item.wait_recv()

    p2_copy = [
        copy(p2out.at[rows_of(j)], p2in.at[rows_of(j)], p_s.at[0, j], p_r.at[0, j], seq=z - 1)
        for j in range(CHUNKS)
    ]
    p1_copy = [
        copy(p1out.at[rows_of(j)], p1in.at[rows_of(j)], p_s.at[1, j], p_r.at[1, j], seq=z - 1)
        for j in range(CHUNKS)
    ]
    tile = 256
    for j in range(CHUNKS):
        r = rows_of(j)

        @pl.when(z > 1)
        def _():
            far_halo[j].wait_recv()

        def tile_body(n, carry):
            t_cols = pl.ds(pl.multiple_of(n * tile, tile), tile)
            g_cols = pl.ds(pl.multiple_of(chans + n * tile, tile), tile)
            tanh_pre = mm(sig[r], w[0, :, t_cols]) + mm(sig1[r], w[1, :, t_cols])
            tanh_pre = tanh_pre + mm(sig2[r], w[2, :, t_cols])
            gate_pre = mm(sig[r], w[0, :, g_cols]) + mm(sig1[r], w[1, :, g_cols])
            gate_pre = gate_pre + mm(sig2[r], w[2, :, g_cols])
            grad_gated = mm(cot[r], wp[t_cols, :], NT)
            tanh_part = jnp.tanh(tanh_pre)
            gate_part = jax.nn.sigmoid(gate_pre)
            g = (tanh_part * gate_part).astype(BF16)
            gated[r, t_cols] = g
            gatedt[t_cols, r] = g.T
            gp[r, t_cols] = (grad_gated * gate_part * (1.0 - tanh_part * tanh_part)).astype(BF16)
            gp[r, g_cols] = (grad_gated * tanh_part * gate_part * (1.0 - gate_part)).astype(BF16)
            return carry

        lax.fori_loop(0, chans // tile, tile_body, 0)

        @pl.when(below)
        def _():
            p2out[r] = mm(gp[r], w[2], NT).astype(BF16)
            p2_copy[j].start()

    sigt[1] = sig1[...].T
    sigt[2] = sig2[...].T

    order = (3, 0, 2, 1)
    conv_cols = 2 * chans // PIECES
    proj_cols = chans // PIECES
    c_copy, x_copy = {}, {}
    for q in order:
        for k in range(TAPS):
            grads[q, :, k * conv_cols:(k + 1) * conv_cols] = mm(
                sigt[k], gp[:, q * conv_cols:(q + 1) * conv_cols]
            ).astype(BF16)
        grads[q, :, TAPS * conv_cols:] = mm(
            gatedt[...], cot[:, q * proj_cols:(q + 1) * proj_cols]
        ).astype(BF16)
        for o in range(nx):
            e = lax.rem(d + o, nx)
            theirs = pl.ds(pl.multiple_of((e * nc + 1 - c) * part, 16), part)
            c_copy[q, o] = copy(
                grads.at[q, theirs], half_in.at[q, o], c_s.at[q, o], c_r.at[q, o], sub=1 - c
            )
            c_copy[q, o].start()

    for q in order:
        for o in list(range(1, nx)) + [0]:
            c_copy[q, o].wait_recv()
            e = lax.rem(d + o, nx)
            ours = pl.ds(pl.multiple_of(base(e), 16), part)
            summed = grads[q, ours].astype(F32) + half_in[q, o].astype(F32)
            if o == 0:
                share[q] = summed
            else:
                x_out[q, o] = summed.astype(BF16)
                x_copy[q, o] = copy(
                    x_out.at[q, o], x_in.at[q, o], x_s.at[q, o], x_r.at[q, o], dp=e
                )
                x_copy[q, o].start()

    for j in range(CHUNKS):
        r = rows_of(j)

        @pl.when(above)
        def _():
            p2_copy[j].wait_recv()

        @pl.when(below)
        def _():
            p1out[r] = (mm(gp[r], w[1], NT) + p2in[r].astype(F32)).astype(BF16)
            p1_copy[j].start()

    for j in range(CHUNKS):
        r = rows_of(j)
        out[r] = (sig[r].astype(F32) + mm(gated[r], wp[...])).astype(BF16)
    for j in range(CHUNKS):
        r = rows_of(j)
        local_sum = cot[r].astype(F32) + mm(gp[r], w[0], NT)

        @pl.when(above)
        def _():
            p1_copy[j].wait_recv()

        gin[r] = (local_sum + p1in[r].astype(F32)).astype(BF16)

    def take_x(q):
        for o in range(1, nx):
            x_copy[q, o].wait_recv()
            share[q] += x_in[q, o].astype(F32)

    def write_out(q, values):
        for k in range(TAPS):
            gconv[k, :, q * conv_cols:(q + 1) * conv_cols] = values[
                :, k * conv_cols:(k + 1) * conv_cols
            ]
        gproj[:, q * proj_cols:(q + 1) * proj_cols] = values[:, TAPS * conv_cols:]

    if reduce_time:
        up = [
            copy(z_out.at[q], z_below.at[q], zb_s.at[q], zb_r.at[q], seq=z + 1)
            for q in range(PIECES)
        ]
        down = [
            copy(z_out.at[q], z_above.at[q], za_s.at[q], za_r.at[q], seq=z - 1)
            for q in range(PIECES)
        ]

        def send_up(q):
            @pl.when(z < q)
            def _():
                @pl.when(below)
                def _():
                    up[q].wait_recv()
                    z_out[q] = (share[q] + z_below[q].astype(F32)).astype(BF16)

                @pl.when(z == 0)
                def _():
                    z_out[q] = share[q].astype(BF16)

                up[q].start()

        def send_down(q):
            @pl.when(z > q)
            def _():
                @pl.when(above)
                def _():
                    down[q].wait_recv()
                    z_out[q] = (share[q] + z_above[q].astype(F32)).astype(BF16)

                @pl.when(z == nz - 1)
                def _():
                    z_out[q] = share[q].astype(BF16)

                down[q].start()

        take_x(3)
        send_up(3)
        take_x(0)
        send_down(0)
        take_x(2)
        send_up(2)
        take_x(1)
        send_down(1)
        send_up(1)
        send_down(2)

        def total_up(q):
            return copy(total.at[q], total.at[q], tu_s.at[q], t_r.at[q], seq=z + 1)

        def total_down(q):
            return copy(total.at[q], total.at[q], td_s.at[q], t_r.at[q], seq=z - 1)

        for q in range(PIECES):
            @pl.when(z == q)
            def _():
                if q > 0:
                    up[q].wait_recv()
                    share[q] += z_below[q].astype(F32)
                if q < nz - 1:
                    down[q].wait_recv()
                    share[q] += z_above[q].astype(F32)
                total[q] = share[q].astype(BF16)
                if q < nz - 1:
                    total_up(q).start()
                if q > 0:
                    total_down(q).start()

        for distance in range(1, nz):
            @pl.when(z >= distance)
            def _():
                q = z - distance
                total_up(q).wait_recv()

                @pl.when(above)
                def _():
                    total_up(q).start()

            @pl.when(z + distance <= nz - 1)
            def _():
                q = z + distance
                total_down(q).wait_recv()

                @pl.when(below)
                def _():
                    total_down(q).start()

        for q in range(PIECES):
            write_out(q, total[q].astype(F32) * factor)

        for q in range(PIECES):
            @pl.when(z < q)
            def _():
                up[q].wait_send()

            @pl.when(z > q)
            def _():
                down[q].wait_send()

            @pl.when((z >= q) & above)
            def _():
                total_up(q).wait_send()

            @pl.when((z <= q) & below)
            def _():
                total_down(q).wait_send()
    else:
        for q in order:
            take_x(q)
            write_out(q, share[q])

    for item in (
        list(wx.values()) + list(wy.values()) + list(wc.values())
        + list(c_copy.values()) + list(x_copy.values())
    ):
        item.wait_send()

    @pl.when(above)
    def _():
        for j in range(CHUNKS):
            own_halo[j].wait_send()

    @pl.when(below & above)
    def _():
        for j in range(CHUNKS):
            far_halo[j].wait_send()

    @pl.when(below)
    def _():
        for j in range(CHUNKS):
            p2_copy[j].wait_send()
            p1_copy[j].wait_send()


def local(sizes, signal, conv_weight, proj_weight, cotangent):
    ny, nz, nx, nc = sizes
    rows, chans = signal.shape[1:]
    assert rows == DILATION and nc == 2 and ny == 2 and signal.shape[0] == 1
    part = conv_weight.shape[0]
    factor = 1.0 / math.sqrt(rows * nz * nx * nc)
    width = (TAPS * 2 * chans + chans) // PIECES
    dma = pltpu.SemaphoreType.DMA
    vmem = pltpu.VMEM
    block = vmem((rows, chans), BF16)
    piece = vmem((PIECES, part, width), BF16)
    scratch = [
        block, block,
        vmem((TAPS, chans, rows), BF16), vmem((chans, rows), BF16),
        vmem((TAPS, chans, 2 * chans), BF16), block, vmem((rows, 2 * chans), BF16), block,
        block, block, block, block,
        vmem((PIECES, chans, width), BF16),
        vmem((PIECES, nx, part, width), BF16),
        vmem((PIECES, nx, part, width), BF16),
        vmem((PIECES, nx, part, width), BF16),
        vmem((PIECES, part, width), F32),
        piece, piece, piece, piece,
    ] + [dma((2, CHUNKS))] * 2 + [dma((TAPS + 1, nx))] * 4 + [dma((TAPS + 1, nx, 2))] * 2 \
        + [dma((2, CHUNKS))] * 2 + [dma((PIECES, nx))] * 4 + [dma((PIECES,))] * 7
    spec = pl.BlockSpec(memory_space=pltpu.VMEM)
    output, grad_input, conv, proj = pl.pallas_call(
        functools.partial(layer_kernel, sizes, factor),
        out_shape=(
            jax.ShapeDtypeStruct((rows, chans), BF16),
            jax.ShapeDtypeStruct((rows, chans), BF16),
            jax.ShapeDtypeStruct((TAPS, part, 2 * chans), F32),
            jax.ShapeDtypeStruct((part, chans), F32),
        ),
        in_specs=[spec] * 4,
        out_specs=(spec,) * 4,
        scratch_shapes=scratch,
        compiler_params=pltpu.CompilerParams(
            collective_id=0, has_side_effects=True, vmem_limit_bytes=48 * 1024 * 1024
        ),
        cost_estimate=pl.CostEstimate(
            flops=22 * rows * chans * chans, bytes_accessed=8 << 20, transcendentals=2 * rows * chans
        ),
    )(signal[0], jnp.swapaxes(conv_weight, 0, 1), proj_weight, cotangent[0])
    conv = jnp.swapaxes(conv, 0, 1)
    if nz != PIECES:
        conv, proj = lax.psum((conv, proj), "seq")
        conv, proj = conv * factor, proj * factor
    return output[None], grad_input[None], conv, proj


def solution(mesh):
    sizes = tuple(mesh.shape[name] for name in ("groups", "seq", "dp", "sub"))
    rows_split = P(("groups", "dp", "sub"), "seq", None)
    return jax.shard_map(
        functools.partial(local, sizes),
        mesh=mesh,
        in_specs=(rows_split, P(("dp", "sub"), None, None), P(("dp", "sub"), None), rows_split),
        out_specs=(
            rows_split,
            rows_split,
            P(("groups", "dp", "sub"), None, None),
            P(("groups", "dp", "sub"), None),
        ),
        check_vma=False,
    )
```

```python
import functools
import math

import jax
import jax.numpy as jnp
from jax import lax
from jax.experimental import pallas as pl
from jax.experimental.pallas import tpu as pltpu
from jax.sharding import PartitionSpec as P

DILATION = 512
TAPS = 3
PIECES = 4
CHUNKS = 4
OWE_LAG = 2
HALVES = 4
LAG_TOTAL = 2
LAG_ON = 5
MESH = pl.DeviceIdType.MESH
F32 = jnp.float32
BF16 = jnp.bfloat16
NN = (((1,), (0,)), ((), ()))
NT = (((1,), (1,)), ((), ()))


def mm(a, b, dims=NN):
    return lax.dot_general(a, b, dims, preferred_element_type=F32)


def layer_kernel(
    sizes, factor,
    sig_hbm, cw, pw, cot_hbm,
    out, gin, gconv, gproj,
    sig, cot, gin_sum, sig1, sig2, sigt, gatedt, w, wp, gp, gated,
    p2in, p1in, p2out, p1out,
    grads, half_in, x_out, x_in, share, z_out, z_below, z_above, total,
    halo_s, halo_r, wx_s, wx_r, wy_s, wy_r, wc_s, wc_r,
    p_s, p_r, c_s, c_r, x_s, x_r, zb_s, zb_r, za_s, za_r, tu_s, td_s, t_r, local_s,
):
    ny, nz, nx, nc = sizes
    h, z, d, c = (lax.axis_index(name) for name in ("groups", "seq", "dp", "sub"))
    rows, chans = sig.shape
    part = cw.shape[1]
    cut = part // ny
    step = rows // CHUNKS
    reduce_time = nz == PIECES
    below, above = z > 0, z < nz - 1

    def copy(src, dst, send, recv, **where):
        return pltpu.make_async_remote_copy(
            src_ref=src, dst_ref=dst, send_sem=send, recv_sem=recv,
            device_id=where, device_id_type=MESH,
        )

    part_at = pl.ds(pl.multiple_of((d * nc + c) * part, 16), part)
    staged = [
        pltpu.make_async_copy(sig_hbm, sig, local_s.at[0]),
        pltpu.make_async_copy(cw, w.at[:, part_at], local_s.at[1]),
        pltpu.make_async_copy(pw, wp.at[part_at], local_s.at[2]),
        pltpu.make_async_copy(cot_hbm, cot, local_s.at[3]),
    ]
    for item in staged:
        item.start()
    barrier = pltpu.get_barrier_semaphore()

    def greet(**where):
        pl.semaphore_signal(barrier, inc=1, device_id=where, device_id_type=MESH)

    @pl.when(below)
    def _():
        greet(seq=z - 1)

    @pl.when(above)
    def _():
        greet(seq=z + 1)

    for o in range(1, nx):
        greet(dp=lax.rem(d + o, nx))
    greet(sub=1 - c)
    greet(groups=1 - h)
    pl.semaphore_wait(
        barrier, (nx - 1) + 2 + below.astype(jnp.int32) + above.astype(jnp.int32)
    )

    def rows_of(j):
        return pl.ds(j * step, step)

    own_halo = [
        copy(sig_hbm.at[rows_of(j)], sig1.at[rows_of(j)], halo_s.at[0, j], halo_r.at[0, j], seq=z + 1)
        for j in range(CHUNKS)
    ]
    far_halo = [
        copy(sig1.at[rows_of(j)], sig2.at[rows_of(j)], halo_s.at[1, j], halo_r.at[1, j], seq=z + 1)
        for j in range(CHUNKS)
    ]

    @pl.when(above)
    def _():
        for j in range(CHUNKS):
            own_halo[j].start()

    def shard(k):
        return cw.at[k] if k < TAPS else pw

    def full(k, at, length):
        at = pl.ds(pl.multiple_of(at, 16), length)
        return w.at[k, at] if k < TAPS else wp.at[at]

    def base(dp_index):
        return (dp_index * nc + c) * part

    mine = base(d)
    wx, wy, wc = {}, {}, {}
    for k in range(TAPS + 1):
        for o in range(1, nx):
            wx[k, o] = copy(
                shard(k).at[pl.ds(pl.multiple_of(h * cut, 16), cut)], full(k, mine + h * cut, cut),
                wx_s.at[k, o], wx_r.at[k, o], dp=lax.rem(d + o, nx),
            )
            wx[k, o].start()
    for k in range(TAPS + 1):
        wc[k, 0, 0] = copy(
            shard(k), full(k, mine, part), wc_s.at[k, 0, 0], wc_r.at[k, 0, 0], sub=1 - c
        )
        wc[k, 0, 0].start()

    @pl.when(z == 0)
    def _():
        sig1[...] = jnp.zeros_like(sig1)

    @pl.when(z < 2)
    def _():
        sig2[...] = jnp.zeros_like(sig2)

    @pl.when(z == nz - 1)
    def _():
        p2in[...] = jnp.zeros_like(p2in)
        p1in[...] = jnp.zeros_like(p1in)

    def pass_halo(j):
        @pl.when(below)
        def _():
            own_halo[j].wait_recv()

        @pl.when(below & above)
        def _():
            far_halo[j].start()

    for k in range(TAPS + 1):
        for o in range(1, nx):
            wx[k, o].wait_recv()
            region = full(k, base(lax.rem(d - o + nx, nx)) + h * cut, cut)
            wy[k, o] = copy(region, region, wy_s.at[k, o], wy_r.at[k, o], groups=1 - h)
            wy[k, o].start()
            wc[k, o, 0] = copy(region, region, wc_s.at[k, o, 0], wc_r.at[k, o, 0], sub=1 - c)
            wc[k, o, 0].start()
        if k < CHUNKS:
            pass_halo(k)
    for item in staged:
        item.wait()
    sigt[0] = sig[...].T
    for k in range(TAPS + 1):
        for o in range(1, nx):
            wy[k, o].wait_recv()
            region = full(k, base(lax.rem(d - o + nx, nx)) + (1 - h) * cut, cut)
            wc[k, o, 1] = copy(region, region, wc_s.at[k, o, 1], wc_r.at[k, o, 1], sub=1 - c)
            wc[k, o, 1].start()
    for item in wc.values():
        item.wait_recv()

    p2_copy = [
        copy(p2out.at[rows_of(j)], p2in.at[rows_of(j)], p_s.at[0, j], p_r.at[0, j], seq=z - 1)
        for j in range(CHUNKS)
    ]
    p1_copy = [
        copy(p1out.at[rows_of(j)], p1in.at[rows_of(j)], p_s.at[1, j], p_r.at[1, j], seq=z - 1)
        for j in range(CHUNKS)
    ]
    def owe_next(j):
        r = rows_of(j)

        @pl.when(below & above)
        def _():
            p2_copy[j].wait_recv()

        @pl.when(below)
        def _():
            p1out[r] = (mm(gp[r], w[1], NT) + p2in[r].astype(F32)).astype(BF16)
            p1_copy[j].start()

    tile = 256
    for j in range(CHUNKS):
        r = rows_of(j)

        @pl.when(z > 1)
        def _():
            far_halo[j].wait_recv()

        def tile_body(n, carry):
            t_cols = pl.ds(pl.multiple_of(n * tile, tile), tile)
            g_cols = pl.ds(pl.multiple_of(chans + n * tile, tile), tile)
            tanh_pre = mm(sig[r], w[0, :, t_cols]) + mm(sig1[r], w[1, :, t_cols])
            tanh_pre = tanh_pre + mm(sig2[r], w[2, :, t_cols])
            gate_pre = mm(sig[r], w[0, :, g_cols]) + mm(sig1[r], w[1, :, g_cols])
            gate_pre = gate_pre + mm(sig2[r], w[2, :, g_cols])
            grad_gated = mm(cot[r], wp[t_cols, :], NT)
            tanh_part = jnp.tanh(tanh_pre)
            gate_part = jax.nn.sigmoid(gate_pre)
            g = (tanh_part * gate_part).astype(BF16)
            gated[r, t_cols] = g
            gatedt[t_cols, r] = g.T
            gp[r, t_cols] = (grad_gated * gate_part * (1.0 - tanh_part * tanh_part)).astype(BF16)
            gp[r, g_cols] = (grad_gated * tanh_part * gate_part * (1.0 - gate_part)).astype(BF16)
            return carry

        lax.fori_loop(0, chans // tile, tile_body, 0)

        @pl.when(z > 1)
        def _():
            p2out[r] = mm(gp[r], w[2], NT).astype(BF16)
            p2_copy[j].start()

        if j >= OWE_LAG:
            owe_next(j - OWE_LAG)

    sigt[1] = sig1[...].T
    sigt[2] = sig2[...].T

    conv_cols = 2 * chans // PIECES
    proj_cols = chans // PIECES
    sub = part // HALVES
    c_copy, x_copy = {}, {}

    def weight_grads(q):
        for k in range(TAPS):
            grads[q, :, k * conv_cols:(k + 1) * conv_cols] = mm(
                sigt[k], gp[:, q * conv_cols:(q + 1) * conv_cols]
            ).astype(BF16)
        grads[q, :, TAPS * conv_cols:] = mm(
            gatedt[...], cot[:, q * proj_cols:(q + 1) * proj_cols]
        ).astype(BF16)
        for o in list(range(1, nx)) + [0]:
            e = lax.rem(d + o, nx)
            theirs = pl.ds(pl.multiple_of((e * nc + 1 - c) * part, 16), part)
            c_copy[q, o] = copy(
                grads.at[q, theirs], half_in.at[q, o], c_s.at[q, o], c_r.at[q, o], sub=1 - c
            )
            c_copy[q, o].start()

    def sum_pair(q):
        for o in list(range(1, nx)) + [0]:
            c_copy[q, o].wait_recv()
            e = lax.rem(d + o, nx)
            ours = pl.ds(pl.multiple_of(base(e), 16), part)
            summed = grads[q, ours].astype(F32) + half_in[q, o].astype(F32)
            if o == 0:
                share[q] = summed
            else:
                x_out[q, o] = summed.astype(BF16)
                for f in range(HALVES):
                    at = pl.ds(f * sub, sub)
                    x_copy[q, o, f] = copy(
                        x_out.at[q, o, at], x_in.at[q, o, at],
                        x_s.at[q, o, f], x_r.at[q, o, f], dp=e,
                    )
                    x_copy[q, o, f].start()

    for q in range(PIECES):
        weight_grads(q)
        if q > 0:
            sum_pair(q - 1)
    sum_pair(PIECES - 1)
    for j in range(CHUNKS - OWE_LAG, CHUNKS):
        owe_next(j)
    for j in range(CHUNKS):
        r = rows_of(j)
        out[r] = (sig[r].astype(F32) + mm(gated[r], wp[...])).astype(BF16)
        gin_sum[r] = cot[r].astype(F32) + mm(gp[r], w[0], NT)

    def take_x(q, f):
        at = pl.ds(f * sub, sub)
        for o in range(1, nx):
            x_copy[q, o, f].wait_recv()
            share[q, at] += x_in[q, o, at].astype(F32)

    def finish_input():
        for j in range(CHUNKS):
            r = rows_of(j)

            @pl.when(above)
            def _():
                p1_copy[j].wait_recv()

            gin[r] = (gin_sum[r] + p1in[r].astype(F32)).astype(BF16)

    def write_out(q, values):
        for k in range(TAPS):
            gconv[k, :, q * conv_cols:(q + 1) * conv_cols] = values[
                :, k * conv_cols:(k + 1) * conv_cols
            ]
        gproj[:, q * proj_cols:(q + 1) * proj_cols] = values[:, TAPS * conv_cols:]

    if reduce_time:
        units = [(q, f) for q in range(PIECES) for f in range(HALVES)]

        def unit(ref, q, f):
            return ref.at[q, pl.ds(f * sub, sub)]

        def up(q, f):
            return copy(
                unit(z_out, q, f), unit(z_below, q, f), zb_s.at[q, f], zb_r.at[q, f], seq=z + 1
            )

        def down(q, f):
            return copy(
                unit(z_out, q, f), unit(z_above, q, f), za_s.at[q, f], za_r.at[q, f], seq=z - 1
            )

        def total_up(q, f):
            return copy(
                unit(total, q, f), unit(total, q, f), tu_s.at[q, f], t_r.at[q, f], seq=z + 1
            )

        def total_down(q, f):
            return copy(
                unit(total, q, f), unit(total, q, f), td_s.at[q, f], t_r.at[q, f], seq=z - 1
            )

        def gather_in(q, f):
            at = pl.ds(f * sub, sub)
            owner = 2
            take_x(q, f)

            @pl.when((z < owner) & below)
            def _():
                up(q, f).wait_recv()
                share[q, at] += z_below[q, at].astype(F32)

            @pl.when((z > owner) & above)
            def _():
                down(q, f).wait_recv()
                share[q, at] += z_above[q, at].astype(F32)

            @pl.when(z != owner)
            def _():
                z_out[q, at] = share[q, at].astype(BF16)

            @pl.when(z < owner)
            def _():
                up(q, f).start()

            @pl.when(z > owner)
            def _():
                down(q, f).start()

        def finish_total(q, f):
            at = pl.ds(f * sub, sub)

            @pl.when(z == 2)
            def _():
                up(q, f).wait_recv()
                down(q, f).wait_recv()
                total[q, at] = (
                    share[q, at] + z_below[q, at].astype(F32) + z_above[q, at].astype(F32)
                ).astype(BF16)
                total_up(q, f).start()
                total_down(q, f).start()

        def hand_on(q, f):
            owner = 2

            @pl.when((z < owner) & below)
            def _():
                total_down(q, f).wait_recv()
                total_down(q, f).start()

            @pl.when((z > owner) & above)
            def _():
                total_up(q, f).wait_recv()
                total_up(q, f).start()

        for i in range(len(units) + LAG_ON):
            if i < len(units):
                gather_in(*units[i])
            if 0 <= i - LAG_TOTAL < len(units):
                finish_total(*units[i - LAG_TOTAL])
            if 0 <= i - LAG_ON < len(units):
                hand_on(*units[i - LAG_ON])

        finish_input()
        for q in range(PIECES):
            for f in range(HALVES):
                @pl.when(z == 0)
                def _():
                    total_down(q, f).wait_recv()

                @pl.when(z == nz - 1)
                def _():
                    total_up(q, f).wait_recv()

            write_out(q, total[q].astype(F32) * factor)

        for q, f in units:
            owner = 2

            @pl.when(z < owner)
            def _():
                up(q, f).wait_send()

            @pl.when(z > owner)
            def _():
                down(q, f).wait_send()

            @pl.when((z >= owner) & above)
            def _():
                total_up(q, f).wait_send()

            @pl.when((z <= owner) & below)
            def _():
                total_down(q, f).wait_send()
    else:
        finish_input()
        for q in range(PIECES):
            for f in range(HALVES):
                take_x(q, f)
            write_out(q, share[q])

    for item in (
        list(wx.values()) + list(wy.values()) + list(wc.values())
        + list(c_copy.values()) + list(x_copy.values())
    ):
        item.wait_send()

    @pl.when(above)
    def _():
        for j in range(CHUNKS):
            own_halo[j].wait_send()

    @pl.when(below & above)
    def _():
        for j in range(CHUNKS):
            far_halo[j].wait_send()

    @pl.when(below)
    def _():
        for j in range(CHUNKS):
            p1_copy[j].wait_send()

    @pl.when(z > 1)
    def _():
        for j in range(CHUNKS):
            p2_copy[j].wait_send()


def local(sizes, signal, conv_weight, proj_weight, cotangent):
    ny, nz, nx, nc = sizes
    rows, chans = signal.shape[1:]
    assert rows == DILATION and nc == 2 and ny == 2 and signal.shape[0] == 1
    part = conv_weight.shape[0]
    factor = 1.0 / math.sqrt(rows * nz * nx * nc)
    width = (TAPS * 2 * chans + chans) // PIECES
    dma = pltpu.SemaphoreType.DMA
    vmem = pltpu.VMEM
    block = vmem((rows, chans), BF16)
    piece = vmem((PIECES, part, width), BF16)
    scratch = [
        block, block, vmem((rows, chans), F32), block, block,
        vmem((TAPS, chans, rows), BF16), vmem((chans, rows), BF16),
        vmem((TAPS, chans, 2 * chans), BF16), block, vmem((rows, 2 * chans), BF16), block,
        block, block, block, block,
        vmem((PIECES, chans, width), BF16),
        vmem((PIECES, nx, part, width), BF16),
        vmem((PIECES, nx, part, width), BF16),
        vmem((PIECES, nx, part, width), BF16),
        vmem((PIECES, part, width), F32),
        piece, piece, piece, piece,
    ] + [dma((2, CHUNKS))] * 2 + [dma((TAPS + 1, nx))] * 4 + [dma((TAPS + 1, nx, 2))] * 2 \
        + [dma((2, CHUNKS))] * 2 + [dma((PIECES, nx))] * 2 + [dma((PIECES, nx, HALVES))] * 2 \
        + [dma((PIECES, HALVES))] * 7 + [dma((4,))]
    spec = pl.BlockSpec(memory_space=pltpu.VMEM)
    anywhere = pl.BlockSpec(memory_space=pl.ANY)
    output, grad_input, conv, proj = pl.pallas_call(
        functools.partial(layer_kernel, sizes, factor),
        out_shape=(
            jax.ShapeDtypeStruct((rows, chans), BF16),
            jax.ShapeDtypeStruct((rows, chans), BF16),
            jax.ShapeDtypeStruct((TAPS, part, 2 * chans), F32),
            jax.ShapeDtypeStruct((part, chans), F32),
        ),
        in_specs=[anywhere] * 4,
        out_specs=(spec,) * 4,
        scratch_shapes=scratch,
        compiler_params=pltpu.CompilerParams(
            collective_id=0, has_side_effects=True, vmem_limit_bytes=56 * 1024 * 1024
        ),
        cost_estimate=pl.CostEstimate(
            flops=22 * rows * chans * chans, bytes_accessed=8 << 20, transcendentals=2 * rows * chans
        ),
    )(signal[0], jnp.swapaxes(conv_weight, 0, 1), proj_weight, cotangent[0])
    conv = jnp.swapaxes(conv, 0, 1)
    if nz != PIECES:
        conv, proj = lax.psum((conv, proj), "seq")
        conv, proj = conv * factor, proj * factor
    return output[None], grad_input[None], conv, proj


def solution(mesh):
    sizes = tuple(mesh.shape[name] for name in ("groups", "seq", "dp", "sub"))
    rows_split = P(("groups", "dp", "sub"), "seq", None)
    return jax.shard_map(
        functools.partial(local, sizes),
        mesh=mesh,
        in_specs=(rows_split, P(("dp", "sub"), None, None), P(("dp", "sub"), None), rows_split),
        out_specs=(
            rows_split,
            rows_split,
            P(("groups", "dp", "sub"), None, None),
            P(("groups", "dp", "sub"), None),
        ),
        check_vma=False,
    )
```
